32 devices in a mesh: slab: 8 (over y, x, core), pencil: 4 (over z).
Axes of the slice: x: 2, y: 2, z: 4, core: 2. Of those that a mesh axis runs over, the one named last changes fastest.
Arguments:
- adjoint_vort: float32 [3, 16, 512, 512], P(None, 'slab', 'pencil'), may hold values from -6 to 6
- omega_ckpt: float32 [2, 3, 16, 512, 512], P(None, None, 'slab', 'pencil'), may hold values from -6 to 6
- cell_shift: int32 [2, 16, 512, 512], P(None, 'slab', 'pencil'), may hold values from -2 to 2
- move_count: int32 [2, 8, 4, 2], P(None, 'slab', 'pencil'), may hold values from 32 to 256, as said below
- move_blocks: int32 [2, 8, 4, 2, 256], P(None, 'slab', 'pencil'), may hold values from 0 to 511, as said below
Outputs:
- adjoint_out: float32 [3, 16, 512, 512], P(None, 'slab', 'pencil')
The draws below stay inside these ranges and needn't reach their ends.
Inputs may be any that keep to these rules, and one draw needn't show every extreme that they name: `move_count`: in every substep and direction some device has 256 live entries and some device 256 // 8. `move_blocks`: for each substep and device, the 512 entries are the plane-block numbers 0 to 511, each once.
All inputs are finite; a program needn't handle non-finite values.
Results may differ from the reference program's by a relative error of at most 0.00025.
Values sent between devices are 32-bit elements; how exact they have to be, the bound alone decides.
A program may use at most 64 MiB of HBM per device.

```python
import math
import jax
import jax.numpy as jnp

NY = 512
NZ = 512
BL = 128
S = 2
CX = 2
SLABS = 8
PENCILS = 4
NX = 16
YP = 128
PLANE_BLOCKS = 512
MOST = 256


def draw_move_count(key, part):
    base_key, heavy_key, start_key = jax.random.split(jax.random.fold_in(key, 11), 3)
    count_shape = (S, SLABS, PENCILS, 2)
    quiet_counts = jax.random.randint(base_key, count_shape, MOST // 8, MOST // 4 + 1, dtype=jnp.int32)
    heavy_counts = jax.random.randint(heavy_key, count_shape, MOST // 2, MOST + 1, dtype=jnp.int32)
    anchor = jax.random.randint(start_key, (), 0, SLABS, dtype=jnp.int32)
    slab_index = jnp.arange(SLABS, dtype=jnp.int32)[None, :, None, None]
    pencil_index = jnp.arange(PENCILS, dtype=jnp.int32)[None, None, :, None]
    distance = (slab_index - anchor) % SLABS
    counts = jnp.where(distance < max(SLABS // 4, 1), heavy_counts, quiet_counts)
    counts = jnp.where((distance == 0) & (pencil_index == 0), MOST, counts)
    counts = jnp.where((distance == SLABS // 2) & (pencil_index == 0), MOST // 8, counts)
    return counts.astype(jnp.int32)


def draw_move_blocks(key, part):
    draw_count = S * SLABS * PENCILS
    item_keys = jax.random.split(jax.random.fold_in(key, 7), draw_count)
    orders = jax.vmap(lambda item_key: jax.random.permutation(item_key, PLANE_BLOCKS))(item_keys)
    return orders.reshape(S, SLABS, PENCILS, 2, MOST).astype(jnp.int32)


def place_ends(array, stream_key, smallest, top_value):
    longest = array.shape.index(max(array.shape))
    spots = []
    for shift in (0, 1):
        where = [jax.random.randint(jax.random.fold_in(stream_key, axis), (), 0, length) for axis, length in enumerate(array.shape)]
        where[longest] = (where[longest] + shift) % array.shape[longest]
        spots.append(tuple(where))
    return array.at[spots[0]].set(smallest).at[spots[1]].set(top_value)


def levels(own_key, extent, pieces, low, largest):
    loudness, own = 1.0, jax.random.fold_in(own_key, 6)
    for axis_at, blocks in pieces:
        steps = jnp.exp(jax.random.uniform(jax.random.fold_in(own, axis_at), (blocks,), jnp.float32, low / len(pieces), largest / len(pieces)))
        loudness = loudness * jnp.repeat(steps, extent[axis_at] // blocks).reshape([-1 if axis == axis_at else 1 for axis in range(len(extent))])
    return loudness


def gaussian(key, shape, spread, most, cuts=(), held_as=jnp.bfloat16):
    factor_of = levels(key, shape, cuts, -0.22, 0.18) if cuts else 1.0
    result = jax.random.normal(key, shape, jnp.float32) * spread * factor_of
    return jnp.minimum(jnp.maximum(result, -most), most).astype(held_as)


def setup_inputs(seed: int = 0) -> dict:
    arg_keys = jax.random.split(jax.random.key(seed), 6)
    return {
        "adjoint_vort": gaussian(arg_keys[0], (3, NX, NY, NZ), 1.0, 6.0, ((1, 8), (2, 4)), jnp.float32),
        "omega_ckpt": gaussian(arg_keys[1], (S, 3, NX, NY, NZ), 1.0, 6.0, ((2, 8), (3, 4)), jnp.float32),
        "cell_shift": place_ends(jax.random.randint(arg_keys[2], (S, NX, NY, NZ), -2, 3), jax.random.fold_in(arg_keys[2], 1), -2, 2).astype(jnp.int32),
        "move_count": draw_move_count(jax.random.fold_in(arg_keys[5], 71), 0),
        "move_blocks": draw_move_blocks(jax.random.fold_in(arg_keys[5], 71), 0),
    }


time_step = 0.25


def cross_product(first_vec, second_vec):
    return jnp.stack([
        first_vec[1] * second_vec[2] - first_vec[2] * second_vec[1],
        first_vec[2] * second_vec[0] - first_vec[0] * second_vec[2],
        first_vec[0] * second_vec[1] - first_vec[1] * second_vec[0],
    ], 0)


def remesh(adjoint, vorticity, shifts, counts, blocks):
    per_row = NZ // BL
    slab_index = jnp.arange(SLABS, dtype=jnp.int32)[:, None, None]
    pencil_index = jnp.arange(PENCILS, dtype=jnp.int32)[None, :, None]
    slot_index = jnp.arange(MOST, dtype=jnp.int32)[None, None, :]
    offsets = jnp.zeros((NX, NY, per_row), jnp.int32)
    for direction, plane_index, step_value in ((0, CX - 1, 1), (1, 0, -1)):
        chosen = blocks[:, :, direction, :]
        alive_slot = slot_index < counts[:, :, direction][:, :, None]
        plane_x = jnp.where(alive_slot, slab_index * CX + plane_index + 0 * chosen, NX).astype(jnp.int32)
        row_y = (pencil_index * YP + chosen // per_row).astype(jnp.int32)
        block_z = (chosen % per_row).astype(jnp.int32)
        offsets = offsets.at[plane_x, row_y, block_z].set(step_value, mode="drop")
    offsets = jnp.repeat(offsets, BL, axis=2)
    x_index = jnp.arange(NX, dtype=jnp.int32)[:, None, None]
    y_index = jnp.arange(NY, dtype=jnp.int32)[None, :, None]
    z_index = jnp.arange(NZ, dtype=jnp.int32)[None, None, :]
    target_x = (x_index + offsets) % NX
    target_z = (z_index + shifts) % NZ
    flat_cell = ((target_x * NY + y_index) * NZ + target_z).reshape(-1).astype(jnp.int32)
    carried = jnp.concatenate([adjoint, vorticity], 0).reshape(6, -1)
    deposit = jnp.zeros((6, NX * NY * NZ), jnp.float32).at[:, flat_cell].add(carried)
    deposit = deposit.reshape(6, NX, NY, NZ)
    return deposit[:3], deposit[3:]


def y_diff(values):
    return (jnp.roll(values, -1, 1) - jnp.roll(values, 1, 1)) * 0.5


def z_diff(values):
    return (jnp.roll(values, -1, 2) - jnp.roll(values, 1, 2)) * 0.5


def velocity(source):
    wave_y = jnp.arange(NY, dtype=jnp.int32)
    wave_z = jnp.arange(NZ, dtype=jnp.int32)
    sine_y = jnp.sin(math.pi * wave_y.astype(jnp.float32) / NY)
    sine_z = jnp.sin(math.pi * wave_z.astype(jnp.float32) / NZ)
    symbol = 4.0 * sine_y[:, None] ** 2 + 4.0 * sine_z[None, :] ** 2
    nonzero = (wave_y[:, None] + wave_z[None, :]) > 0
    factor = jnp.where(nonzero, 1.0 / jnp.where(nonzero, symbol, 1.0), 0.0)
    spectrum = jnp.fft.fft2(source, axes=(-2, -1))
    stream = jnp.real(jnp.fft.ifft2(spectrum * factor, axes=(-2, -1))).astype(jnp.float32)
    first_part = y_diff(stream[2]) - z_diff(stream[1])
    second = z_diff(stream[0])
    third_part = -y_diff(stream[0])
    return jnp.stack([first_part, second, third_part], 0)


def reference(adjoint_vort, omega_ckpt, cell_shift, move_count, move_blocks):
    adjoint = adjoint_vort
    for substep in range(S):
        remeshed, vortex = remesh(adjoint, omega_ckpt[substep], cell_shift[substep], move_count[substep], move_blocks[substep])
        velocity_field = velocity(remeshed)
        slope_x = (jnp.roll(velocity_field, -1, 1) - jnp.roll(velocity_field, 1, 1)) * 0.5
        adjoint = remeshed + time_step * (cross_product(vortex, velocity_field) + vortex[0] * slope_x)
    return adjoint
```

```python
import jax
import jax.numpy as jnp
import numpy as np
from jax import lax
from jax.sharding import PartitionSpec as P

BL = 128


time_step = 0.25
high = lax.Precision.HIGH


def shifted(value, axis, by):
    count = lax.axis_size(axis)
    return lax.ppermute(value, axis, [(i, (i + by) % count) for i in range(count)])


def padded_2(cells, sides, width):
    for axis, dim in sides:
        count = lax.axis_size(axis)
        head = lax.slice_in_dim(cells, 0, width, axis=dim)
        tail = lax.slice_in_dim(cells, cells.shape[dim] - width, cells.shape[dim], axis=dim)
        cells = jnp.concatenate(
            [
                lax.ppermute(tail, axis, [(i, (i + 1) % count) for i in range(count)]),
                cells,
                lax.ppermute(head, axis, [((i + 1) % count, i) for i in range(count)]),
            ],
            axis=dim,
        )
    return cells


def cross_product(first_vec, second_vec):
    return jnp.stack(
        [
            first_vec[1] * second_vec[2] - first_vec[2] * second_vec[1],
            first_vec[2] * second_vec[0] - first_vec[0] * second_vec[2],
            first_vec[0] * second_vec[1] - first_vec[1] * second_vec[0],
        ],
        0,
    )


def tables(rows, groups, depth):
    k = np.arange(depth)
    phase = 2.0 * np.pi * ((k[:, None] * k[None, :]) % depth) / depth
    cas = np.cos(phase) + np.sin(phase)
    slope = np.sin(2.0 * np.pi * k / depth)[:, None] * (np.cos(phase) - np.sin(phase))
    ev_z = 4.0 * np.sin(np.pi * k / depth) ** 2
    j = np.arange(1, rows + 1)
    norm = np.sqrt(2.0 / (rows + 1))
    sine = norm * np.sin(np.pi * j[:, None] * j[None, :] / (rows + 1))
    ghost = np.zeros((rows + 2, rows))
    ghost[1:-1] = sine
    dsine = 0.5 * (ghost[2:] - ghost[:-2])
    ev_y = 4.0 * np.sin(np.pi * j / (2.0 * (rows + 1))) ** 2
    inverse = 1.0 / (ev_y[:, None] + ev_z[None, :])
    decay = np.exp(-2.0 * np.arcsinh(np.sqrt(ev_z[1:]) / 2.0))[None, :]
    y = np.arange(-1, rows + 1)[:, None]
    left = np.zeros((rows + 2, depth))
    left[:, 0] = (rows - y[:, 0]) / (rows + 1.0)
    left[:, 1:] = decay ** (y + 1.0) * (1.0 - decay ** (2.0 * (rows - y))) / (1.0 - decay ** (2.0 * (rows + 1)))
    right = left[::-1]
    quad = np.zeros((rows + 2, depth))
    quad[:, 0] = (y[:, 0] + 1) * (rows - y[:, 0]) / 2.0
    bend = np.stack([left[1:-1], right[1:-1], quad[1:-1]])
    dbend = np.stack([0.5 * (t[2:] - t[:-2]) for t in (left, right, quad)])
    near, far = left[1], left[rows]
    size = 2 * groups
    system = np.tile(np.eye(size), (depth, 1, 1))
    for p in range(groups):
        before, after = 2 * ((p - 1) % groups) + 1, 2 * ((p + 1) % groups)
        system[:, 2 * p, before] -= near
        system[:, 2 * p, after] -= far
        system[:, 2 * p + 1, before] -= far
        system[:, 2 * p + 1, after] -= near
    solve = np.zeros_like(system)
    solve[1:] = np.linalg.inv(system[1:])
    solve[0] = np.linalg.pinv(system[0], rcond=1e-9)
    coef = np.zeros((3, groups, 3, depth))
    for out, row in ((0, 2 * (groups - 1) + 1), (1, 2 * (1 % groups))):
        for q in range(groups):
            coef[out, q, 0] = solve[:, row, 2 * q]
            coef[out, q, 1] = solve[:, row, 2 * q + 1]
            both = solve[0, row, 2 * q] + solve[0, row, 2 * q + 1]
            every = solve[0, row].sum() / groups
            coef[out, q, 2, 0] = (both - every) * rows / 2.0
    coef[2, :, 2, 0] = -1.0 / groups
    coef[2, 0, 2, 0] += 1.0
    return cas, slope, sine, dsine, inverse, bend, dbend, coef


def shifted_deposit(values, shifts):
    total = jnp.zeros(values.shape, jnp.float32)
    for amount in (-2, -1, 0, 1, 2):
        picked = jnp.where(shifts == amount, values, 0.0)
        total = total + jnp.roll(picked, amount, axis=-1)
    return total


def velocity(source):
    planes, rows, depth = source.shape[1:]
    groups = lax.axis_size("pencil")
    cas, slope, sine, dsine, inverse, bend, dbend, coef = [
        jnp.asarray(t, jnp.float32) for t in tables(rows, groups, depth)
    ]
    hat = jnp.einsum("cxyz,zk->cxyk", source, cas, precision=high)
    zero = (jnp.arange(depth) == 0).astype(jnp.float32)
    mean = jnp.mean(hat, axis=2) * zero
    hat = hat - mean[:, :, None]
    modes = jnp.einsum("jy,cxyk->cxjk", sine, hat, precision=high) * inverse
    local = jnp.einsum("yj,cxjk->cxyk", sine, modes, precision=high)
    edges = jnp.stack([local[:, :, 0], local[:, :, rows - 1], mean])
    got = [edges] + [shifted(edges, "pencil", -d) for d in range(1, groups)]
    ghosts = [
        sum(coef[o, q, e] * got[q][e] for q in range(groups) for e in range(3)) for o in range(3)
    ]
    pick = jnp.stack([local[1], local[0]])
    for o in range(3):
        pick = pick + bend[o] * jnp.stack([ghosts[o][1], ghosts[o][0]])[:, :, None]
    tilt = jnp.einsum("yj,cxjk->cxyk", dsine, jnp.stack([modes[2], modes[0]]), precision=high)
    for o in range(3):
        tilt = tilt + dbend[o] * jnp.stack([ghosts[o][2], ghosts[o][0]])[:, :, None]
    plain = jnp.einsum("cxyk,kz->cxyz", tilt, cas / depth, precision=high)
    sloped = jnp.einsum("cxyk,kz->cxyz", pick, slope / depth, precision=high)
    return jnp.stack([plain[0] - sloped[0], sloped[1], -plain[1]], 0)


def shards(adjoint_vort, omega_ckpt, cell_shift, move_count, move_blocks):
    planes = adjoint_vort.shape[1]
    local_rows = adjoint_vort.shape[2]
    depth_cells = adjoint_vort.shape[3]
    per_row = depth_cells // BL
    plane_blocks = local_rows * per_row
    all_blocks = planes * plane_blocks
    capacity = move_blocks.shape[-1]
    block_id = jnp.arange(all_blocks, dtype=jnp.int32)
    slot_id = jnp.arange(capacity, dtype=jnp.int32)

    def cell_mask(block_mask):
        spread = jnp.broadcast_to(
            block_mask.reshape(planes, local_rows, per_row, 1), (planes, local_rows, per_row, BL)
        )
        return spread.reshape(planes, local_rows, depth_cells)

    adjoint = adjoint_vort
    for substep in range(omega_ckpt.shape[0]):
        shifts = cell_shift[substep]
        payload = jnp.concatenate([adjoint, omega_ckpt[substep]], 0)
        chosen = move_blocks[substep, 0, 0]
        alive_slot = slot_id[None, :] < move_count[substep, 0, 0][:, None]
        right_ids = (planes - 1) * plane_blocks + chosen[0]
        left_ids = chosen[1]
        right_hit = jnp.any(
            (block_id[:, None] == right_ids[None, :]) & alive_slot[0][None, :], axis=1
        )
        left_hit = jnp.any(
            (block_id[:, None] == left_ids[None, :]) & alive_slot[1][None, :], axis=1
        )
        right_cells = cell_mask(right_hit)
        left_cells = cell_mask(left_hit)
        staying = jnp.where(right_cells | left_cells, 0.0, payload)
        deposit = shifted_deposit(staying, shifts)
        right_plane = shifted_deposit(
            jnp.where(right_cells[planes - 1], payload[:, planes - 1], 0.0), shifts[planes - 1]
        )
        left_plane = shifted_deposit(jnp.where(left_cells[0], payload[:, 0], 0.0), shifts[0])
        from_left = shifted(right_plane, "slab", 1)
        from_right = shifted(left_plane, "slab", -1)
        deposit = deposit.at[:, 0].add(from_left)
        deposit = deposit.at[:, planes - 1].add(from_right)
        remeshed = deposit[:3]
        vortex = deposit[3:]
        velocity_field = velocity(remeshed)
        padded = padded_2(velocity_field, (("slab", 1),), 1)
        slope_x = (padded[:, 2:] - padded[:, :-2]) * 0.5
        adjoint = remeshed + time_step * (
            cross_product(vortex, velocity_field) + vortex[0] * slope_x
        )
    return adjoint


def solution(mesh):
    return jax.shard_map(
        shards,
        mesh=mesh,
        in_specs=(
            P(None, "slab", "pencil", None),
            P(None, None, "slab", "pencil", None),
            P(None, "slab", "pencil", None),
            P(None, "slab", "pencil", None),
            P(None, "slab", "pencil", None, None),
        ),
        out_specs=P(None, "slab", "pencil", None),
        check_vma=False,
    )
```

```python
import functools

import jax
import jax.numpy as jnp
import ml_dtypes
import numpy as np
from jax import lax
from jax.experimental import pallas as pl
from jax.experimental.pallas import tpu as pltpu
from jax.sharding import PartitionSpec as P

BL = 128
TILE = 16
AWAY = 16
MESH = pl.DeviceIdType.MESH
bf16 = jnp.bfloat16
f32 = jnp.float32

time_step = 0.25


def tables(rows, groups, depth):
    k = np.arange(depth)
    phase = 2.0 * np.pi * ((k[:, None] * k[None, :]) % depth) / depth
    cas = np.cos(phase) + np.sin(phase)
    slope = np.sin(2.0 * np.pi * k / depth)[:, None] * (np.cos(phase) - np.sin(phase))
    ev_z = 4.0 * np.sin(np.pi * k / depth) ** 2
    j = np.arange(1, rows + 1)
    norm = np.sqrt(2.0 / (rows + 1))
    sine = norm * np.sin(np.pi * j[:, None] * j[None, :] / (rows + 1))
    ghost = np.zeros((rows + 2, rows))
    ghost[1:-1] = sine
    dsine = 0.5 * (ghost[2:] - ghost[:-2])
    ev_y = 4.0 * np.sin(np.pi * j / (2.0 * (rows + 1))) ** 2
    inverse = 1.0 / (ev_y[:, None] + ev_z[None, :])
    decay = np.exp(-2.0 * np.arcsinh(np.sqrt(ev_z[1:]) / 2.0))[None, :]
    y = np.arange(-1, rows + 1)[:, None]
    left = np.zeros((rows + 2, depth))
    left[:, 0] = (rows - y[:, 0]) / (rows + 1.0)
    left[:, 1:] = decay ** (y + 1.0) * (1.0 - decay ** (2.0 * (rows - y))) / (1.0 - decay ** (2.0 * (rows + 1)))
    right = left[::-1]
    quad = np.zeros((rows + 2, depth))
    quad[:, 0] = (y[:, 0] + 1) * (rows - y[:, 0]) / 2.0
    bend = np.stack([left[1:-1], right[1:-1], quad[1:-1]])
    dbend = np.stack([0.5 * (t[2:] - t[:-2]) for t in (left, right, quad)])
    near, far = left[1], left[rows]
    size = 2 * groups
    system = np.tile(np.eye(size), (depth, 1, 1))
    for p in range(groups):
        before, after = 2 * ((p - 1) % groups) + 1, 2 * ((p + 1) % groups)
        system[:, 2 * p, before] -= near
        system[:, 2 * p, after] -= far
        system[:, 2 * p + 1, before] -= far
        system[:, 2 * p + 1, after] -= near
    solve = np.zeros_like(system)
    solve[1:] = np.linalg.inv(system[1:])
    solve[0] = np.linalg.pinv(system[0], rcond=1e-9)
    coef = np.zeros((3, groups, 3, depth))
    for out, row in ((0, 2 * (groups - 1) + 1), (1, 2 * (1 % groups))):
        for q in range(groups):
            coef[out, q, 0] = solve[:, row, 2 * q]
            coef[out, q, 1] = solve[:, row, 2 * q + 1]
            both = solve[0, row, 2 * q] + solve[0, row, 2 * q + 1]
            every = solve[0, row].sum() / groups
            coef[out, q, 2, 0] = (both - every) * rows / 2.0
    coef[2, :, 2, 0] = -1.0 / groups
    coef[2, 0, 2, 0] += 1.0
    return cas, slope, sine, dsine, inverse, bend, dbend, coef


def shifted_deposit(values, shifts):
    total = jnp.zeros(values.shape, jnp.float32)
    for amount in (-2, -1, 0, 1, 2):
        picked = jnp.where(shifts == amount, values, 0.0)
        total = total + jnp.roll(picked, amount, axis=-1)
    return total


def split_table(table):
    table = np.asarray(table, np.float32)
    high = table.astype(ml_dtypes.bfloat16)
    low = (table - high.astype(np.float32)).astype(ml_dtypes.bfloat16)
    return high, low


def stacked_table(table):
    high, low = split_table(table)
    top = np.concatenate([high, high], 1)
    return np.concatenate([top, np.concatenate([low, np.zeros_like(low)], 1)], 0)


def split(value):
    high = value.astype(bf16)
    return high, (value - high.astype(f32)).astype(bf16)


def dot(left, right):
    return jnp.dot(left, right, preferred_element_type=f32)


def kernel(
    sizes,
    lists,
    adjoint_in,
    shifts_in,
    ends,
    omega_hbm,
    *refs,
):
    steps, planes, rows, depth, groups, slabs, capacity, count = sizes
    table_hbm = refs[:count]
    out = refs[count]
    table_vmem = refs[count + 1 : 2 * count + 1]
    (
        omega_in,
        code,
        lam,
        current,
        vortex,
        lam_send,
        lam_recv,
        omega_send,
        omega_recv,
        field,
        field_recv,
        edges,
        source_hi,
        source_lo,
        modes,
        spec_hi,
        spec_lo,
        load_sem,
        omega_sem,
        lam_ssem,
        lam_rsem,
        omega_ssem,
        omega_rsem,
        field_ssem,
        field_rsem,
        edge_ssem,
        edge_rsem,
    ) = refs[2 * count + 1 :]
    cas_hi, cas_lo, slope_hi, slope_lo, sine, dsine, inverse, bend, dbend, coef = table_vmem
    slab = lax.axis_index("slab")
    pencil = lax.axis_index("pencil")
    onward = lax.rem(slab + 1, slabs)
    back = lax.rem(slab + slabs - 1, slabs)
    others = [lax.rem(pencil + groups - d, groups) for d in range(1, groups)]

    omega_load = pltpu.make_async_copy(omega_hbm, omega_in, omega_sem.at[0])
    omega_load.start()
    loads = [
        pltpu.make_async_copy(table_hbm[t], table_vmem[t], load_sem.at[t]) for t in range(count)
    ]
    for load in loads:
        load.start()

    barrier = pltpu.get_barrier_semaphore()
    for target in (onward, back):
        pl.semaphore_signal(barrier, inc=1, device_id={"slab": target}, device_id_type=MESH)
    for target in others:
        pl.semaphore_signal(barrier, inc=1, device_id={"pencil": target}, device_id_type=MESH)

    sent = []

    def send(source, target, ssem, rsem, to):
        copy = pltpu.make_async_remote_copy(
            src_ref=source,
            dst_ref=target,
            send_sem=ssem,
            recv_sem=rsem,
            device_id=to,
            device_id_type=MESH,
        )
        copy.start()
        sent.append(copy)
        return copy

    def make_code(s):
        row_id = lax.broadcasted_iota(jnp.int32, (rows, capacity), 0)
        block_id = lax.broadcasted_iota(jnp.int32, (depth, capacity), 0) >> (BL.bit_length() - 1)
        for direction, x in ((0, planes - 1), (1, 0)):
            at = (s * 2 + direction) * 2
            row_hit = jnp.where(row_id == lists[at : at + 1, :], 1.0, 0.0).astype(bf16)
            block_hit = jnp.where(block_id == lists[at + 1 : at + 2, :], 1.0, 0.0).astype(bf16)
            hit = lax.dot_general(
                row_hit, block_hit, (((1,), (1,)), ((), ())), preferred_element_type=f32
            )
            code[s, x] = shifts_in[s, x] + jnp.where(hit > 0.5, AWAY, 0)

    def deposit(s, values, stay, leave):
        def tile(i, carry):
            at = pl.ds(pl.multiple_of(i * 8, 8), 8)
            for x in range(planes):
                direction = 0 if x == planes - 1 else 1
                mine = code[s, x, at, :]
                carried = [values[c, x, at, :] for c in range(3)]
                kept = [jnp.where(mine == 0, v, 0.0) for v in carried]
                gone = [jnp.where(mine == AWAY, v, 0.0) for v in carried]
                for amount in (-2, -1, 1, 2):
                    turned = pltpu.roll(mine, amount % depth, 1)
                    here = turned == amount
                    there = turned == amount + AWAY
                    for c in range(3):
                        moved = pltpu.roll(carried[c], amount % depth, 1)
                        kept[c] = kept[c] + jnp.where(here, moved, 0.0)
                        gone[c] = gone[c] + jnp.where(there, moved, 0.0)
                for c in range(3):
                    stay[c, x, at, :] = kept[c]
                    leave[direction, c, at, :] = gone[c]
            return carry

        lax.fori_loop(0, rows // 8, tile, 0)

    def send_lam(s):
        copies = []
        for c in range(3):
            copies.append(
                [
                    send(
                        lam_send.at[s, d, c],
                        lam_recv.at[s, d, c],
                        lam_ssem.at[s, d, c],
                        lam_rsem.at[s, d, c],
                        {"slab": (onward, back)[d]},
                    )
                    for d in range(2)
                ]
            )
        return copies

    def send_omega(s):
        return [
            send(
                omega_send.at[s, d],
                omega_recv.at[s, d],
                omega_ssem.at[s, d],
                omega_rsem.at[s, d],
                {"slab": (onward, back)[d]},
            )
            for d in range(2)
        ]

    make_code(0)
    deposit(0, adjoint_in, lam, lam_send.at[0])
    pl.semaphore_wait(barrier, 2 + groups - 1)
    lam_copies = send_lam(0)
    omega_load.wait()
    deposit(0, omega_in.at[0], vortex.at[0], omega_send.at[0])
    omega_copies = send_omega(0)
    for load in loads:
        load.wait()

    first = (lax.broadcasted_iota(jnp.int32, (1, depth), 1) == 0).astype(f32)
    for s in range(steps):
        edges[s, 0] = jnp.zeros((3, 8, depth), f32)
        for c in range(3):
            for copy in lam_copies[c]:
                copy.wait_recv()

            def gather(i, carry):
                at = pl.ds(pl.multiple_of(i * TILE, TILE), TILE)
                for x in range(planes):
                    total = lam[c, x, at, :]
                    if x == 0:
                        total = total + lam_recv[s, 0, c, at, :]
                    if x == planes - 1:
                        total = total + lam_recv[s, 1, c, at, :]
                    lam[c, x, at, :] = total
                    high, low = split(total)
                    to = pl.ds(pl.multiple_of(x * rows + i * TILE, TILE), TILE)
                    source_hi[to, :] = high
                    source_lo[to, :] = low
                return carry

            lax.fori_loop(0, rows // TILE, gather, 0)
            hat = (
                dot(source_hi[...], cas_hi[...])
                + dot(source_lo[...], cas_hi[...])
                + dot(source_hi[...], cas_lo[...])
            )
            for x in range(planes):
                part = hat[x * rows : (x + 1) * rows]
                mean = jnp.sum(part, axis=0, keepdims=True) * (first / rows)
                high, low = split(part - mean)
                wide = dot(sine[...], jnp.concatenate([high, low], 0))
                amount = (wide[:rows] + wide[rows:]) * inverse[...]
                n = c * planes + x
                for e in range(2):
                    edges[s, 0, e, n : n + 1, :] = jnp.sum(
                        amount * ends[:, e : e + 1], axis=0, keepdims=True
                    )
                edges[s, 0, 2, n : n + 1, :] = mean
                high, low = split(amount)
                modes[n, :rows, :] = high
                modes[n, rows:, :] = low
        edge_copies = [
            send(
                edges.at[s, 0],
                edges.at[s, d],
                edge_ssem.at[s, d - 1],
                edge_rsem.at[s, d - 1],
                {"pencil": others[d - 1]},
            )
            for d in range(1, groups)
        ]
        for copy in edge_copies:
            copy.wait_recv()
        ghosts = []
        for o in range(3):
            total = jnp.zeros((8, depth), f32)
            for q in range(groups):
                for e in range(3):
                    total = total + coef[o, q, e : e + 1, :] * edges[s, q, e]
            ghosts.append(total)
        for slot, c, matrix, shape in (
            (0, 2, dsine, dbend),
            (1, 0, dsine, dbend),
            (2, 1, sine, bend),
            (3, 0, sine, bend),
        ):
            for x in range(planes):
                n = c * planes + x
                wide = dot(matrix[...], modes[n])
                value = wide[:rows] + wide[rows:]
                for o in range(3):
                    value = value + shape[o] * ghosts[o][n : n + 1]
                high, low = split(value)
                spec_hi[slot, x * rows : (x + 1) * rows, :] = high
                spec_lo[slot, x * rows : (x + 1) * rows, :] = low

        def along_z(slot, hi, lo):
            return (
                dot(spec_hi[slot], hi[...])
                + dot(spec_lo[slot], hi[...])
                + dot(spec_hi[slot], lo[...])
            )

        field_copies = []
        scale = 1.0 / depth
        for c in (1, 2, 0):
            if c == 1:
                got = along_z(3, slope_hi, slope_lo) * scale
            elif c == 2:
                got = along_z(1, cas_hi, cas_lo) * -scale
            else:
                got = (along_z(0, cas_hi, cas_lo) - along_z(2, slope_hi, slope_lo)) * scale
            for x in range(planes):
                field[s, c, x] = got[x * rows : (x + 1) * rows]
            for d, x in ((0, planes - 1), (1, 0)):
                field_copies.append(
                    send(
                        field.at[s, c, x],
                        field_recv.at[s, d, c],
                        field_ssem.at[s, d, c],
                        field_rsem.at[s, d, c],
                        {"slab": (onward, back)[d]},
                    )
                )
        arriving = omega_copies
        if s + 1 < steps:
            make_code(s + 1)
            deposit(s + 1, omega_in.at[s + 1], vortex.at[s + 1], omega_send.at[s + 1])
            omega_copies = send_omega(s + 1)
        for copy in arriving:
            copy.wait_recv()
        for copy in field_copies:
            copy.wait_recv()
        result = current if s + 1 < steps else out

        def update(i, carry):
            at = pl.ds(pl.multiple_of(i * 8, 8), 8)
            for x in range(planes):
                w = [vortex[s, c, x, at, :] for c in range(3)]
                if x == 0:
                    w = [w[c] + omega_recv[s, 0, c, at, :] for c in range(3)]
                if x == planes - 1:
                    w = [w[c] + omega_recv[s, 1, c, at, :] for c in range(3)]
                g = [field[s, c, x, at, :] for c in range(3)]
                crossed = (
                    w[1] * g[2] - w[2] * g[1],
                    w[2] * g[0] - w[0] * g[2],
                    w[0] * g[1] - w[1] * g[0],
                )
                for c in range(3):
                    if x == 0:
                        low = field_recv[s, 0, c, at, :]
                    else:
                        low = field[s, c, x - 1, at, :]
                    if x == planes - 1:
                        high = field_recv[s, 1, c, at, :]
                    else:
                        high = field[s, c, x + 1, at, :]
                    slope_x = (high - low) * 0.5
                    result[c, x, at, :] = lam[c, x, at, :] + time_step * (
                        crossed[c] + w[0] * slope_x
                    )
            return carry

        lax.fori_loop(0, rows // 8, update, 0)
        if s + 1 < steps:
            deposit(s + 1, current, lam, lam_send.at[s + 1])
            lam_copies = send_lam(s + 1)
    for copy in sent:
        copy.wait_send()


def shards(adjoint_vort, omega_ckpt, cell_shift, move_count, move_blocks):
    _, planes, rows, depth = adjoint_vort.shape
    steps = omega_ckpt.shape[0]
    groups, slabs = lax.axis_size("pencil"), lax.axis_size("slab")
    capacity = move_blocks.shape[-1]
    assert planes == 2
    per_row = depth // BL
    chosen = move_blocks[:, 0, 0]
    alive = jnp.arange(capacity, dtype=jnp.int32) < move_count[:, 0, 0][..., None]
    lists = jnp.stack([jnp.where(alive, chosen // per_row, -1), chosen % per_row], 2)
    lists = lists.reshape(steps * 4, capacity)

    cas, slope, sine, dsine, inverse, bend, dbend, coef = tables(rows, groups, depth)
    ends = np.zeros((rows, 128), np.float32)
    ends[:, 0], ends[:, 1] = sine[0], sine[-1]
    held = [
        *split_table(cas),
        *split_table(slope),
        stacked_table(sine),
        stacked_table(dsine),
        np.asarray(inverse, np.float32),
        np.asarray(bend, np.float32),
        np.asarray(dbend, np.float32),
        np.asarray(coef, np.float32),
    ]
    held = [jnp.asarray(t) for t in held]
    count = len(held)
    dma = pltpu.SemaphoreType.DMA
    vm = pltpu.VMEM
    scratch = [vm(t.shape, t.dtype) for t in held] + [
        vm(omega_ckpt.shape, f32),
        vm((steps, planes, rows, depth), jnp.int32),
        vm((3, planes, rows, depth), f32),
        vm((3, planes, rows, depth), f32),
        vm((steps, 3, planes, rows, depth), f32),
        vm((steps, 2, 3, rows, depth), f32),
        vm((steps, 2, 3, rows, depth), f32),
        vm((steps, 2, 3, rows, depth), f32),
        vm((steps, 2, 3, rows, depth), f32),
        vm((steps, 3, planes, rows, depth), f32),
        vm((steps, 2, 3, rows, depth), f32),
        vm((steps, groups, 3, 8, depth), f32),
        vm((planes * rows, depth), bf16),
        vm((planes * rows, depth), bf16),
        vm((3 * planes, 2 * rows, depth), bf16),
        vm((4, planes * rows, depth), bf16),
        vm((4, planes * rows, depth), bf16),
        dma((count,)),
        dma((1,)),
        dma((steps, 2, 3)),
        dma((steps, 2, 3)),
        dma((steps, 2)),
        dma((steps, 2)),
        dma((steps, 2, 3)),
        dma((steps, 2, 3)),
        dma((steps, groups - 1)),
        dma((steps, groups - 1)),
    ]
    sizes = (steps, planes, rows, depth, groups, slabs, capacity, count)
    local = pl.BlockSpec(memory_space=pltpu.VMEM)
    return pl.pallas_call(
        functools.partial(kernel, sizes),
        out_shape=jax.ShapeDtypeStruct(adjoint_vort.shape, f32),
        in_specs=[local] * 4 + [pl.BlockSpec(memory_space=pl.ANY)] * (1 + count),
        out_specs=local,
        scratch_shapes=scratch,
        compiler_params=pltpu.CompilerParams(
            collective_id=0, has_side_effects=True, vmem_limit_bytes=56 * 1024 * 1024
        ),
    )(lists, adjoint_vort, cell_shift, jnp.asarray(ends), omega_ckpt, *held)


def solution(mesh):
    return jax.shard_map(
        shards,
        mesh=mesh,
        in_specs=(
            P(None, "slab", "pencil", None),
            P(None, None, "slab", "pencil", None),
            P(None, "slab", "pencil", None),
            P(None, "slab", "pencil", None),
            P(None, "slab", "pencil", None, None),
        ),
        out_specs=P(None, "slab", "pencil", None),
        check_vma=False,
    )
```

```python
import functools

import jax
import jax.numpy as jnp
import ml_dtypes
import numpy as np
from jax import lax
from jax.experimental import pallas as pl
from jax.experimental.pallas import tpu as pltpu
from jax.sharding import PartitionSpec as P

BL = 128
TILE = 16
AWAY = 16
MESH = pl.DeviceIdType.MESH
bf16 = jnp.bfloat16
f32 = jnp.float32

time_step = 0.25


def tables(rows, groups, depth):
    k = np.arange(depth)
    phase = 2.0 * np.pi * ((k[:, None] * k[None, :]) % depth) / depth
    cas = np.cos(phase) + np.sin(phase)
    slope = np.sin(2.0 * np.pi * k / depth)[:, None] * (np.cos(phase) - np.sin(phase))
    ev_z = 4.0 * np.sin(np.pi * k / depth) ** 2
    j = np.arange(1, rows + 1)
    norm = np.sqrt(2.0 / (rows + 1))
    sine = norm * np.sin(np.pi * j[:, None] * j[None, :] / (rows + 1))
    ghost = np.zeros((rows + 2, rows))
    ghost[1:-1] = sine
    dsine = 0.5 * (ghost[2:] - ghost[:-2])
    ev_y = 4.0 * np.sin(np.pi * j / (2.0 * (rows + 1))) ** 2
    inverse = 1.0 / (ev_y[:, None] + ev_z[None, :])
    decay = np.exp(-2.0 * np.arcsinh(np.sqrt(ev_z[1:]) / 2.0))[None, :]
    y = np.arange(-1, rows + 1)[:, None]
    left = np.zeros((rows + 2, depth))
    left[:, 0] = (rows - y[:, 0]) / (rows + 1.0)
    left[:, 1:] = decay ** (y + 1.0) * (1.0 - decay ** (2.0 * (rows - y))) / (1.0 - decay ** (2.0 * (rows + 1)))
    right = left[::-1]
    quad = np.zeros((rows + 2, depth))
    quad[:, 0] = (y[:, 0] + 1) * (rows - y[:, 0]) / 2.0
    bend = np.stack([left[1:-1], right[1:-1], quad[1:-1]])
    dbend = np.stack([0.5 * (t[2:] - t[:-2]) for t in (left, right, quad)])
    near, far = left[1], left[rows]
    size = 2 * groups
    system = np.tile(np.eye(size), (depth, 1, 1))
    for p in range(groups):
        before, after = 2 * ((p - 1) % groups) + 1, 2 * ((p + 1) % groups)
        system[:, 2 * p, before] -= near
        system[:, 2 * p, after] -= far
        system[:, 2 * p + 1, before] -= far
        system[:, 2 * p + 1, after] -= near
    solve = np.zeros_like(system)
    solve[1:] = np.linalg.inv(system[1:])
    solve[0] = np.linalg.pinv(system[0], rcond=1e-9)
    coef = np.zeros((3, groups, 3, depth))
    for out, row in ((0, 2 * (groups - 1) + 1), (1, 2 * (1 % groups))):
        for q in range(groups):
            coef[out, q, 0] = solve[:, row, 2 * q]
            coef[out, q, 1] = solve[:, row, 2 * q + 1]
            both = solve[0, row, 2 * q] + solve[0, row, 2 * q + 1]
            every = solve[0, row].sum() / groups
            coef[out, q, 2, 0] = (both - every) * rows / 2.0
    coef[2, :, 2, 0] = -1.0 / groups
    coef[2, 0, 2, 0] += 1.0
    return cas, slope, sine, dsine, inverse, bend, dbend, coef


def shifted_deposit(values, shifts):
    total = jnp.zeros(values.shape, jnp.float32)
    for amount in (-2, -1, 0, 1, 2):
        picked = jnp.where(shifts == amount, values, 0.0)
        total = total + jnp.roll(picked, amount, axis=-1)
    return total


def split_table(table):
    table = np.asarray(table, np.float32)
    high = table.astype(ml_dtypes.bfloat16)
    low = (table - high.astype(np.float32)).astype(ml_dtypes.bfloat16)
    return high, low


def stacked_table(table):
    high, low = split_table(table)
    top = np.concatenate([high, high], 1)
    return np.concatenate([top, np.concatenate([low, np.zeros_like(low)], 1)], 0)


def split(value):
    high = value.astype(bf16)
    return high, (value - high.astype(f32)).astype(bf16)


def dot(left, right):
    return jnp.dot(left, right, preferred_element_type=f32)


def kernel(
    sizes,
    lists,
    lists_t,
    adjoint_in,
    shifts_in,
    ends,
    omega_hbm,
    *refs,
):
    steps, planes, rows, depth, groups, slabs, capacity, count = sizes
    table_hbm = refs[:count]
    out = refs[count]
    table_vmem = refs[count + 1 : 2 * count + 1]
    (
        omega_in,
        code,
        lam,
        current,
        vortex,
        lam_send,
        lam_recv,
        omega_send,
        omega_recv,
        field,
        field_recv,
        edges,
        source_hi,
        source_lo,
        modes,
        spec_hi,
        spec_lo,
        load_sem,
        omega_sem,
        lam_ssem,
        lam_rsem,
        omega_ssem,
        omega_rsem,
        field_ssem,
        field_rsem,
        edge_ssem,
        edge_rsem,
        shift_send,
        shift_recv,
        lists_recv,
        lam_in,
        omega_new,
        packed_hi,
        packed_lo,
        shift_ssem,
        shift_rsem,
        lists_ssem,
        lists_rsem,
    ) = refs[2 * count + 1 :]
    cas_hi, cas_lo, slope_hi, slope_lo, sine, dsine, inverse, bend, dbend, coef = table_vmem
    slab = lax.axis_index("slab")
    pencil = lax.axis_index("pencil")
    onward = lax.rem(slab + 1, slabs)
    back = lax.rem(slab + slabs - 1, slabs)
    others = [lax.rem(pencil + groups - d, groups) for d in range(1, groups)]

    omega_load = pltpu.make_async_copy(omega_hbm, omega_in, omega_sem.at[0])
    omega_load.start()
    loads = [
        pltpu.make_async_copy(table_hbm[t], table_vmem[t], load_sem.at[t]) for t in range(count)
    ]
    for load in loads:
        load.start()

    barrier = pltpu.get_barrier_semaphore()
    for target in (onward, back):
        pl.semaphore_signal(barrier, inc=1, device_id={"slab": target}, device_id_type=MESH)
    for target in others:
        pl.semaphore_signal(barrier, inc=1, device_id={"pencil": target}, device_id_type=MESH)

    sent = []

    def send(source, target, ssem, rsem, to):
        copy = pltpu.make_async_remote_copy(
            src_ref=source,
            dst_ref=target,
            send_sem=ssem,
            recv_sem=rsem,
            device_id=to,
            device_id_type=MESH,
        )
        copy.start()
        sent.append(copy)
        return copy

    per_row = depth // BL
    blocks = per_row * rows
    sides = ((0, planes - 1), (1, 0))

    def spread(row):
        block_id = lax.broadcasted_iota(jnp.int32, (blocks, capacity), 0)
        return jnp.where(block_id == row, 1.0, 0.0).astype(bf16)

    def make_code(s):
        ones = jnp.ones((capacity, BL), bf16)
        for d, x in sides:
            hit = dot(spread(lists[s * 2 + d : s * 2 + d + 1, :]), ones)
            for b in range(per_row):
                lanes = slice(b * BL, (b + 1) * BL)
                away = jnp.where(hit[b * rows : (b + 1) * rows] > 0.5, AWAY, 0)
                code[s, x, :, lanes] = shifts_in[s, x, :, lanes] + away

    def stacked(plane):
        return jnp.concatenate([plane[:, b * BL : (b + 1) * BL] for b in range(per_row)], 0)

    def chooser(s, d):
        block_id = lax.broadcasted_iota(jnp.int32, (capacity, blocks), 1)
        column = lists_t[:, s * 2 + d : s * 2 + d + 1]
        return jnp.where(block_id == column, 1.0, 0.0).astype(bf16)

    def pack(s, values, leave):
        for d, x in sides:
            choose = chooser(s, d)
            for c in range(3):
                high, low = split(stacked(values[c, x]))
                leave[d, :, c * BL : (c + 1) * BL] = dot(choose, high) + dot(choose, low)

    def pack_shift(s):
        for d, x in sides:
            moved = stacked(shifts_in[s, x]).astype(f32).astype(bf16)
            shift_send[s, d] = dot(chooser(s, d), moved)

    def unpack(s, arrived, target):
        for d in range(2):

            def tile(i, carry):
                at = pl.ds(pl.multiple_of(i * TILE, TILE), TILE)
                amounts = shift_recv[s, d, at, :]
                lane = lax.broadcasted_iota(jnp.int32, (TILE, BL), 1)
                carried = [arrived[s, d, at, c * BL : (c + 1) * BL] for c in range(3)]
                inside = [jnp.where(amounts == 0.0, v, 0.0) for v in carried]
                across = [jnp.zeros((TILE, BL), f32) for v in carried]
                for amount in (-2, -1, 1, 2):
                    here = pltpu.roll(amounts, amount % BL, 1) == float(amount)
                    wraps = lane < amount if amount > 0 else lane >= BL + amount
                    for c in range(3):
                        moved = jnp.where(here, pltpu.roll(carried[c], amount % BL, 1), 0.0)
                        inside[c] = inside[c] + jnp.where(wraps, 0.0, moved)
                        across[c] = across[c] + jnp.where(wraps, moved, 0.0)
                for c in range(3):
                    for part, value in ((0, inside[c]), (1, across[c])):
                        high, low = split(value)
                        lanes = slice((2 * c + part) * BL, (2 * c + part + 1) * BL)
                        packed_hi[at, lanes] = high
                        packed_lo[at, lanes] = low
                return carry

            lax.fori_loop(0, capacity // TILE, tile, 0)
            place = spread(lists_recv[d, s * 2 + d : s * 2 + d + 1, :])
            lower = lax.broadcasted_iota(jnp.int32, (rows, BL), 1) < BL // 2
            for c in range(3):
                lanes = slice(2 * c * BL, 2 * (c + 1) * BL)
                full = dot(place, packed_hi[:, lanes]) + dot(place, packed_lo[:, lanes])

                def piece(b, part):
                    b = b % per_row
                    return full[b * rows : (b + 1) * rows, part * BL : (part + 1) * BL]

                for b in range(per_row):
                    target[d, c, :, b * BL : (b + 1) * BL] = piece(b, 0) + jnp.where(
                        lower, piece(b - 1, 1), piece(b + 1, 1)
                    )

    def deposit(s, values, stay):
        def tile(i, carry):
            at = pl.ds(pl.multiple_of(i * 8, 8), 8)
            for x in range(planes):
                mine = code[s, x, at, :]
                carried = [values[c, x, at, :] for c in range(3)]
                kept = [jnp.where(mine == 0, v, 0.0) for v in carried]
                for amount in (-2, -1, 1, 2):
                    turned = pltpu.roll(mine, amount % depth, 1)
                    here = turned == amount
                    for c in range(3):
                        moved = pltpu.roll(carried[c], amount % depth, 1)
                        kept[c] = kept[c] + jnp.where(here, moved, 0.0)
                for c in range(3):
                    stay[c, x, at, :] = kept[c]
            return carry

        lax.fori_loop(0, rows // 8, tile, 0)

    def send_sides(s, source, target, ssem, rsem):
        return [
            send(
                source.at[s, d],
                target.at[s, d],
                ssem.at[s, d],
                rsem.at[s, d],
                {"slab": (onward, back)[d]},
            )
            for d in range(2)
        ]

    def send_lam(s):
        return send_sides(s, lam_send, lam_recv, lam_ssem, lam_rsem)

    def send_omega(s):
        return send_sides(s, omega_send, omega_recv, omega_ssem, omega_rsem)

    def send_shift(s):
        return send_sides(s, shift_send, shift_recv, shift_ssem, shift_rsem)

    pack(0, adjoint_in, lam_send.at[0])
    pack_shift(0)
    pl.semaphore_wait(barrier, 2 + groups - 1)
    list_copies = [
        send(
            lists,
            lists_recv.at[d],
            lists_ssem.at[d],
            lists_rsem.at[d],
            {"slab": (onward, back)[d]},
        )
        for d in range(2)
    ]
    shift_copies = send_shift(0)
    lam_copies = send_lam(0)
    make_code(0)
    omega_load.wait()
    pack(0, omega_in.at[0], omega_send.at[0])
    omega_copies = send_omega(0)
    deposit(0, adjoint_in, lam)
    deposit(0, omega_in.at[0], vortex.at[0])
    for load in loads:
        load.wait()
    for copy in list_copies:
        copy.wait_recv()

    first = (lax.broadcasted_iota(jnp.int32, (1, depth), 1) == 0).astype(f32)
    for s in range(steps):
        edges[s, 0] = jnp.zeros((3, 8, depth), f32)
        for copy in shift_copies:
            copy.wait_recv()
        for copy in lam_copies:
            copy.wait_recv()
        unpack(s, lam_recv, lam_in)
        for c in range(3):

            def gather(i, carry):
                at = pl.ds(pl.multiple_of(i * TILE, TILE), TILE)
                for x in range(planes):
                    total = lam[c, x, at, :]
                    if x == 0:
                        total = total + lam_in[0, c, at, :]
                    if x == planes - 1:
                        total = total + lam_in[1, c, at, :]
                    lam[c, x, at, :] = total
                    high, low = split(total)
                    to = pl.ds(pl.multiple_of(x * rows + i * TILE, TILE), TILE)
                    source_hi[to, :] = high
                    source_lo[to, :] = low
                return carry

            lax.fori_loop(0, rows // TILE, gather, 0)
            hat = (
                dot(source_hi[...], cas_hi[...])
                + dot(source_lo[...], cas_hi[...])
                + dot(source_hi[...], cas_lo[...])
            )
            for x in range(planes):
                part = hat[x * rows : (x + 1) * rows]
                mean = jnp.sum(part, axis=0, keepdims=True) * (first / rows)
                high, low = split(part - mean)
                wide = dot(sine[...], jnp.concatenate([high, low], 0))
                amount = (wide[:rows] + wide[rows:]) * inverse[...]
                n = c * planes + x
                for e in range(2):
                    edges[s, 0, e, n : n + 1, :] = jnp.sum(
                        amount * ends[:, e : e + 1], axis=0, keepdims=True
                    )
                edges[s, 0, 2, n : n + 1, :] = mean
                high, low = split(amount)
                modes[n, :rows, :] = high
                modes[n, rows:, :] = low
        edge_copies = [
            send(
                edges.at[s, 0],
                edges.at[s, d],
                edge_ssem.at[s, d - 1],
                edge_rsem.at[s, d - 1],
                {"pencil": others[d - 1]},
            )
            for d in range(1, groups)
        ]
        for copy in edge_copies:
            copy.wait_recv()
        ghosts = []
        for o in range(3):
            total = jnp.zeros((8, depth), f32)
            for q in range(groups):
                for e in range(3):
                    total = total + coef[o, q, e : e + 1, :] * edges[s, q, e]
            ghosts.append(total)
        for slot, c, matrix, shape in (
            (0, 2, dsine, dbend),
            (1, 0, dsine, dbend),
            (2, 1, sine, bend),
            (3, 0, sine, bend),
        ):
            for x in range(planes):
                n = c * planes + x
                wide = dot(matrix[...], modes[n])
                value = wide[:rows] + wide[rows:]
                for o in range(3):
                    value = value + shape[o] * ghosts[o][n : n + 1]
                high, low = split(value)
                spec_hi[slot, x * rows : (x + 1) * rows, :] = high
                spec_lo[slot, x * rows : (x + 1) * rows, :] = low

        def along_z(slot, hi, lo):
            return (
                dot(spec_hi[slot], hi[...])
                + dot(spec_lo[slot], hi[...])
                + dot(spec_hi[slot], lo[...])
            )

        field_copies = []
        scale = 1.0 / depth
        for c in (1, 2, 0):
            if c == 1:
                got = along_z(3, slope_hi, slope_lo) * scale
            elif c == 2:
                got = along_z(1, cas_hi, cas_lo) * -scale
            else:
                got = (along_z(0, cas_hi, cas_lo) - along_z(2, slope_hi, slope_lo)) * scale
            for x in range(planes):
                field[s, c, x] = got[x * rows : (x + 1) * rows]
            for d, x in ((0, planes - 1), (1, 0)):
                field_copies.append(
                    send(
                        field.at[s, c, x],
                        field_recv.at[s, d, c],
                        field_ssem.at[s, d, c],
                        field_rsem.at[s, d, c],
                        {"slab": (onward, back)[d]},
                    )
                )
        arriving = omega_copies
        if s + 1 < steps:
            make_code(s + 1)
            pack_shift(s + 1)
            shift_copies = send_shift(s + 1)
            pack(s + 1, omega_in.at[s + 1], omega_send.at[s + 1])
            omega_copies = send_omega(s + 1)
            deposit(s + 1, omega_in.at[s + 1], vortex.at[s + 1])
        for copy in arriving:
            copy.wait_recv()
        unpack(s, omega_recv, omega_new)
        for copy in field_copies:
            copy.wait_recv()
        result = current if s + 1 < steps else out

        def update(i, carry):
            at = pl.ds(pl.multiple_of(i * 8, 8), 8)
            for x in range(planes):
                w = [vortex[s, c, x, at, :] for c in range(3)]
                if x == 0:
                    w = [w[c] + omega_new[0, c, at, :] for c in range(3)]
                if x == planes - 1:
                    w = [w[c] + omega_new[1, c, at, :] for c in range(3)]
                g = [field[s, c, x, at, :] for c in range(3)]
                crossed = (
                    w[1] * g[2] - w[2] * g[1],
                    w[2] * g[0] - w[0] * g[2],
                    w[0] * g[1] - w[1] * g[0],
                )
                for c in range(3):
                    if x == 0:
                        low = field_recv[s, 0, c, at, :]
                    else:
                        low = field[s, c, x - 1, at, :]
                    if x == planes - 1:
                        high = field_recv[s, 1, c, at, :]
                    else:
                        high = field[s, c, x + 1, at, :]
                    slope_x = (high - low) * 0.5
                    result[c, x, at, :] = lam[c, x, at, :] + time_step * (
                        crossed[c] + w[0] * slope_x
                    )
            return carry

        lax.fori_loop(0, rows // 8, update, 0)
        if s + 1 < steps:
            pack(s + 1, current, lam_send.at[s + 1])
            lam_copies = send_lam(s + 1)
            deposit(s + 1, current, lam)
    for copy in sent:
        copy.wait_send()


def shards(adjoint_vort, omega_ckpt, cell_shift, move_count, move_blocks):
    _, planes, rows, depth = adjoint_vort.shape
    steps = omega_ckpt.shape[0]
    groups, slabs = lax.axis_size("pencil"), lax.axis_size("slab")
    capacity = move_blocks.shape[-1]
    assert planes == 2
    per_row = depth // BL
    chosen = move_blocks[:, 0, 0]
    alive = jnp.arange(capacity, dtype=jnp.int32) < move_count[:, 0, 0][..., None]
    lists = jnp.where(alive, chosen % per_row * rows + chosen // per_row, -1)
    lists = lists.reshape(steps * 2, capacity)

    cas, slope, sine, dsine, inverse, bend, dbend, coef = tables(rows, groups, depth)
    ends = np.zeros((rows, 128), np.float32)
    ends[:, 0], ends[:, 1] = sine[0], sine[-1]
    held = [
        *split_table(cas),
        *split_table(slope),
        stacked_table(sine),
        stacked_table(dsine),
        np.asarray(inverse, np.float32),
        np.asarray(bend, np.float32),
        np.asarray(dbend, np.float32),
        np.asarray(coef, np.float32),
    ]
    held = [jnp.asarray(t) for t in held]
    count = len(held)
    dma = pltpu.SemaphoreType.DMA
    vm = pltpu.VMEM
    scratch = [vm(t.shape, t.dtype) for t in held] + [
        vm(omega_ckpt.shape, f32),
        vm((steps, planes, rows, depth), jnp.int32),
        vm((3, planes, rows, depth), f32),
        vm((3, planes, rows, depth), f32),
        vm((steps, 3, planes, rows, depth), f32),
        vm((steps, 2, capacity, 3 * BL), f32),
        vm((steps, 2, capacity, 3 * BL), f32),
        vm((steps, 2, capacity, 3 * BL), f32),
        vm((steps, 2, capacity, 3 * BL), f32),
        vm((steps, 3, planes, rows, depth), f32),
        vm((steps, 2, 3, rows, depth), f32),
        vm((steps, groups, 3, 8, depth), f32),
        vm((planes * rows, depth), bf16),
        vm((planes * rows, depth), bf16),
        vm((3 * planes, 2 * rows, depth), bf16),
        vm((4, planes * rows, depth), bf16),
        vm((4, planes * rows, depth), bf16),
        dma((count,)),
        dma((1,)),
        dma((steps, 2)),
        dma((steps, 2)),
        dma((steps, 2)),
        dma((steps, 2)),
        dma((steps, 2, 3)),
        dma((steps, 2, 3)),
        dma((steps, groups - 1)),
        dma((steps, groups - 1)),
        vm((steps, 2, capacity, BL), f32),
        vm((steps, 2, capacity, BL), f32),
        vm((2, steps * 2, capacity), jnp.int32),
        vm((2, 3, rows, depth), f32),
        vm((2, 3, rows, depth), f32),
        vm((capacity, 6 * BL), bf16),
        vm((capacity, 6 * BL), bf16),
        dma((steps, 2)),
        dma((steps, 2)),
        dma((2,)),
        dma((2,)),
    ]
    sizes = (steps, planes, rows, depth, groups, slabs, capacity, count)
    local = pl.BlockSpec(memory_space=pltpu.VMEM)
    return pl.pallas_call(
        functools.partial(kernel, sizes),
        out_shape=jax.ShapeDtypeStruct(adjoint_vort.shape, f32),
        in_specs=[local] * 5 + [pl.BlockSpec(memory_space=pl.ANY)] * (1 + count),
        out_specs=local,
        scratch_shapes=scratch,
        compiler_params=pltpu.CompilerParams(
            collective_id=0, has_side_effects=True, vmem_limit_bytes=56 * 1024 * 1024
        ),
    )(lists, lists.T, adjoint_vort, cell_shift, jnp.asarray(ends), omega_ckpt, *held)


def solution(mesh):
    return jax.shard_map(
        shards,
        mesh=mesh,
        in_specs=(
            P(None, "slab", "pencil", None),
            P(None, None, "slab", "pencil", None),
            P(None, "slab", "pencil", None),
            P(None, "slab", "pencil", None),
            P(None, "slab", "pencil", None, None),
        ),
        out_specs=P(None, "slab", "pencil", None),
        check_vma=False,
    )
```
